256 devices in a mesh: rows: 32 (over x, z), cols: 8 (over y, core).
Axes of the slice: x: 4, y: 4, z: 8, core: 2. Of those that a mesh axis runs over, the one named last changes fastest.
Arguments:
- weight: bfloat16 [8192, 28672], P('cols', 'rows'), may hold values from -0.6 to 0.6
- calib: bfloat16 [2048, 8192], P('rows', 'cols'), may hold values from -180 to 180
- sketch: bfloat16 [28672, 256], P('rows'), may hold values from -6 to 6
Outputs:
- sparse: bfloat16 [8192, 28672], P('cols', 'rows')
- basis: bfloat16 [8192, 256], P('cols')
- coeffs: bfloat16 [256, 28672], P(None, 'rows')
- out_error: float32 [2048, 28672], P('cols', 'rows')
The draws below stay inside these ranges and needn't reach their ends.
All inputs are finite; a program needn't handle non-finite values.
Results may differ from the reference program's by a relative error of at most 0.023.
Values may be sent and summed in bfloat16 or wider, within the bound.
A program may use at most 64 MiB of HBM per device.

```python
import jax
import jax.numpy as jnp
from jax import lax

D = 8192
F = 28672
K = 256
CAL = 2048


def draw_weight(key, part):
    key = jax.random.fold_in(key, 11)
    noise = jnp.clip(jax.random.normal(key, (D, F), jnp.float32), -6.0, 6.0)
    rowf = 1.0 + 2.0 * jnp.arange(D, dtype=jnp.float32)[:, None] / D
    colf = 1.0 + 2.0 * jnp.arange(F, dtype=jnp.float32)[None, :] / F
    return jnp.clip(noise * rowf * colf / 91.0, -0.6, 0.6).astype(jnp.bfloat16)


def draw_calib(key, part):
    key = jax.random.fold_in(key, 23)
    colkey = jax.random.fold_in(key, 1)
    colscale = jnp.exp(jax.random.uniform(colkey, (1, D), jnp.float32, 0.0, 2.3))
    rowf = 1.0 + 2.0 * jnp.arange(CAL, dtype=jnp.float32)[:, None] / CAL
    noise = jnp.clip(jax.random.normal(key, (CAL, D), jnp.float32), -6.0, 6.0)
    return (noise * colscale * rowf).astype(jnp.bfloat16)


def level_of(key, dims, cuts, least, largest):
    gain, own = 1.0, jax.random.fold_in(key, 6)
    for dim, parts in cuts:
        heights = jnp.exp(jax.random.uniform(jax.random.fold_in(own, dim), (parts,), jnp.float32, least / len(cuts), largest / len(cuts)))
        gain = gain * jnp.repeat(heights, dims[dim] // parts).reshape([-1 if axis == dim else 1 for axis in range(len(dims))])
    return gain


def normal_values(key, shape, scale, reach, cuts=(), kind=jnp.bfloat16):
    level = level_of(key, shape, cuts, -0.22, 0.18) if cuts else 1.0
    array = jax.random.normal(key, shape, jnp.float32) * scale * level
    return jnp.minimum(jnp.maximum(array, -reach), reach).astype(kind)


def setup_inputs(seed: int = 0) -> dict:
    key_of = jax.random.split(jax.random.key(seed), 4)
    return {
        "weight": draw_weight(jax.random.fold_in(key_of[3], 71), 0),
        "calib": draw_calib(jax.random.fold_in(key_of[3], 71), 0),
        "sketch": normal_values(key_of[2], (F, K), 1.0, 6.0, ((0, 32),)),
    }


def reference(weight, calib, sketch):
    xval = calib.astype(jnp.float32)
    scale = jnp.sqrt(lax.optimization_barrier(jnp.sum(xval * xval, axis=0)) / CAL + 1e-06)
    blocks = 8
    width = F // blocks
    total = jnp.float32(0.0)
    for blk in range(blocks):
        scaled = scale[:, None] * weight[:, blk * width:(blk + 1) * width].astype(jnp.float32)
        total = total + jnp.sum(jnp.abs(scaled))
    tau = 2.0 * total / (D * F)
    sparse_parts = []
    resid_parts = []
    ranged = jnp.zeros((D, K), jnp.float32)
    for blk in range(blocks):
        scaled = scale[:, None] * weight[:, blk * width:(blk + 1) * width].astype(jnp.float32)
        clipped = jnp.clip(scaled, -tau, tau)
        sparse_parts.append((scaled - clipped).astype(jnp.bfloat16))
        resid = clipped.astype(jnp.bfloat16)
        resid_parts.append(resid)
        ranged = ranged + jnp.dot(resid.astype(jnp.float32), sketch[blk * width:(blk + 1) * width].astype(jnp.float32), preferred_element_type=jnp.float32)
    gram = jnp.dot(ranged.T, ranged, precision=lax.Precision.HIGHEST)
    chol = jnp.linalg.cholesky(gram)
    basis = jax.scipy.linalg.solve_triangular(chol, ranged.T, lower=True).T.astype(jnp.bfloat16)
    xs = (xval / scale[None, :]).astype(jnp.bfloat16)
    coeff_parts = []
    error_parts = []
    for blk in range(blocks):
        resid = resid_parts[blk]
        coeff = lax.dot_general(basis.astype(jnp.float32), resid.astype(jnp.float32), (((0,), (0,)), ((), ())), preferred_element_type=jnp.float32).astype(jnp.bfloat16)
        coeff_parts.append(coeff)
        err = (resid.astype(jnp.float32) - jnp.dot(basis.astype(jnp.float32), coeff.astype(jnp.float32), preferred_element_type=jnp.float32)).astype(jnp.bfloat16)
        error_parts.append(jnp.dot(xs.astype(jnp.float32), err.astype(jnp.float32), preferred_element_type=jnp.float32))
    return (jnp.concatenate(sparse_parts, axis=1), basis, jnp.concatenate(coeff_parts, axis=1), jnp.concatenate(error_parts, axis=1))
```

```python
import jax
import jax.numpy as jnp
from jax import lax
from jax.experimental import pallas as pl
from jax.experimental.pallas import tpu as pltpu
from jax.sharding import PartitionSpec as P

MESH = pl.DeviceIdType.MESH
F32, BF16 = jnp.float32, jnp.bfloat16
NX, NZ, NY = 4, 8, 4
RANK = 256
PANEL = 32


def split3(v):
    a = v.astype(BF16)
    rest = v - a.astype(F32)
    b = rest.astype(BF16)
    return a, b, (rest - b.astype(F32)).astype(BF16)


def split2(v):
    a = v.astype(BF16)
    return a, (v - a.astype(F32)).astype(BF16)


def dot(a, b, ca, cb):
    return lax.dot_general(a, b, (((ca,), (cb,)), ((), ())), preferred_element_type=F32)


def inverse_factor(m_ref, out_ref):
    lane = lax.broadcasted_iota(jnp.int32, (PANEL, 2 * RANK), 1)
    sub8 = lax.broadcasted_iota(jnp.int32, (8, 128), 0)
    groups = PANEL // 8

    def panel(step, carry):
        k0 = pl.multiple_of(step * PANEL, PANEL)
        rows = m_ref[pl.ds(k0, PANEL), :]
        rows = jnp.where(lane >= k0, rows, 0.0)
        diag = pltpu.roll(rows[:, :RANK], lax.rem(RANK - k0, RANK), 1)[:, :128]
        rg = [rows[8 * g:8 * g + 8, :] for g in range(groups)]
        dg = [diag[8 * g:8 * g + 8, :] for g in range(groups)]
        for q in range(groups):
            left = range(groups - q)
            col = [
                [jnp.broadcast_to(dg[g][:, 8 * q + j:8 * q + j + 1], (8, 128)) for g in range(q, groups)]
                for j in range(8)
            ]
            pivots = jnp.zeros((8, 128), F32)
            for j in range(8):
                pivot = jnp.broadcast_to(col[j][0][j:j + 1, :], (8, 128))
                inv = 1.0 / pivot
                pivots = jnp.where(sub8 == j, pivot, pivots)
                mult = [col[j][g] * inv for g in left]
                mult[0] = jnp.where(sub8 > j, mult[0], 0.0)
                for other in range(j + 1, 8):
                    row = jnp.broadcast_to(col[other][0][j:j + 1, :], (8, 128))
                    for g in left:
                        col[other][g] = col[other][g] - mult[g] * row
                rrow, drow = rg[q][j:j + 1, :], dg[q][j:j + 1, :]
                for g in left:
                    rg[q + g] = rg[q + g] - jnp.concatenate([mult[g]] * 4, axis=1) * rrow
                    dg[q + g] = dg[q + g] - mult[g] * drow
            root = lax.rsqrt(pivots)
            rg[q] = rg[q] * jnp.concatenate([root] * 4, axis=1)
        done = jnp.concatenate(rg, axis=0)
        out_ref[pl.ds(k0, PANEL), :] = done[:, RANK:]
        a, b, c = split3(done)
        lhs = jnp.concatenate([a, a, b, a, b, c], axis=0)[:, :RANK]
        rhs = jnp.concatenate([a, b, a, c, b, a], axis=0)
        m_ref[...] -= dot(lhs, rhs, 0, 0)
        return carry

    lax.fori_loop(0, RANK // PANEL, panel, 0)


def exchange_kernel(
    w_ref, cal_in, sk_ref,
    a_out, q_out, linv_out, rng, z_out, scale_out, tau_out,
    cal, stx, stx_in, stz, stz_in, tsend, t_in, resid, rclip, rp, rx_in, rzs, rz_in,
    gp, gcore, gs, gy_in, gown, gfull, zp, zcore, zs, zy_in, qp, qcore, qs, qy_in, ap, acore, asum, ay_in, m_ref, rscaled,
    ssem, rsem,
):
    rr, cc = lax.axis_index("rows"), lax.axis_index("cols")
    x, z = rr // NZ, lax.rem(rr, NZ)
    y, k = cc // 2, lax.rem(cc, 2)
    sib = 1 - k

    def xat(d):
        return lax.rem(x + d, NX)

    def zat(d):
        return lax.rem(z + d, NZ)

    def yat(d):
        return lax.rem(y + d, NY)

    def dev(xx=x, zz=z, yy=y, kk=k):
        return (xx * NZ + zz, yy * 2 + kk)

    count = [0]
    pending = []

    def send(src, dst, to):
        i = count[0]
        count[0] += 1
        copy = pltpu.make_async_remote_copy(
            src_ref=src, dst_ref=dst, send_sem=ssem.at[i], recv_sem=rsem.at[i], device_id=to, device_id_type=MESH
        )
        copy.start()
        pending.append(copy)
        return copy

    def arrive(copies):
        for copy in copies:
            copy.wait_recv()

    barrier = pltpu.get_barrier_semaphore()
    partners = [dev(xx=xat(d)) for d in range(1, NX)] + [dev(zz=zat(d)) for d in range(1, NZ)]
    partners += [(rr, lax.rem(cc + d, 8)) for d in range(1, 8)]
    for p in partners:
        pl.semaphore_signal(barrier, inc=1, device_id=p, device_id_type=MESH)

    for i in range(2):
        part = cal_in[:, 512 * i:512 * i + 512].astype(F32)
        stx[0:1, 512 * i:512 * i + 512] = jnp.sum(part * part, axis=0, keepdims=True)
    ones = jnp.ones((8, w_ref.shape[1]), BF16)
    for i in range(4):
        stx[1:2, 256 * i:256 * i + 256] = dot(ones, jnp.abs(w_ref[256 * i:256 * i + 256, :]), 1, 1)[0:1, :]
    pl.semaphore_wait(barrier, len(partners))

    sx = [send(stx, stx_in.at[d - 1], dev(xx=xat(d))) for d in range(1, NX)]

    xs_plus, xs_minus, zs_plus, zs_minus = xat(1), xat(NX - 1), zat(1), zat(NZ - 1)
    own = cal.at[x, z]
    own[...] = cal_in[...]

    def h0x1():
        return [send(cal.at[x, z, 0:32], cal.at[x, z, 0:32], dev(xx=xs_plus)),
                send(cal.at[x, z, 0:32], cal.at[x, z, 0:32], dev(xx=xs_minus))]

    def h0x2():
        lo, hi = cal.at[xs_minus, z, 0:16], cal.at[xs_plus, z, 16:32]
        return [send(lo, lo, dev(xx=xs_plus)), send(hi, hi, dev(xx=xs_minus))]

    def h1z(step):
        lo, hi = zat(NZ - step + 1), zat(step - 1)
        tl, th = (slice(32, 64), slice(32, 64)) if step < 4 else (slice(32, 48), slice(48, 64))
        up, down = cal.at[x, lo, tl], cal.at[x, hi, th]
        return [send(up, up, dev(zz=zs_plus)), send(down, down, dev(zz=zs_minus))]

    def h0z(step):
        lo, hi = zat(NZ - step + 1), zat(step - 1)
        tl, th = (slice(0, 32), slice(0, 32)) if step < 4 else (slice(0, 16), slice(16, 32))
        up, down = cal.at[:, lo, tl], cal.at[:, hi, th]
        return [send(up, up, dev(zz=zs_plus)), send(down, down, dev(zz=zs_minus))]

    def h1x1():
        block = cal.at[x, :, 32:64]
        return [send(block, block, dev(xx=xs_plus)), send(block, block, dev(xx=xs_minus))]

    def h1x2():
        lo, hi = cal.at[xs_minus, :, 32:48], cal.at[xs_plus, :, 48:64]
        return [send(lo, lo, dev(xx=xs_plus)), send(hi, hi, dev(xx=xs_minus))]

    g_x, g_z = h0x1(), h1z(1)

    arrive(sx)
    stz[...] = stx[...] + stx_in[0] + stx_in[1] + stx_in[2]
    sz = [send(stz, stz_in.at[d - 1], dev(zz=zat(d))) for d in range(1, NZ)]
    arrive(g_x)
    g_x = h0x2()
    arrive(g_z)
    g_z = h1z(2)
    arrive(sz)
    tot = stz[...]
    for d in range(1, NZ):
        tot = tot + stz_in[d - 1]
    scale_row = jnp.sqrt(tot[0:1, :] / (NX * NZ * cal_in.shape[0]) + 1e-06)
    mine = jnp.sum(scale_row * tot[1:2, :], axis=1, keepdims=True)
    tsend[...] = jnp.broadcast_to(mine, (8, 128))
    st = [send(tsend, t_in.at[d - 1], (rr, lax.rem(cc + d, 8))) for d in range(1, 8)]
    arrive(g_x)
    g_h0z = h0z(1)
    arrive(g_z)
    g_z = h1z(3)
    for i in range(8):
        row = scale_row[:, 128 * i:128 * i + 128]
        scale_out[128 * i:128 * i + 128, :] = jnp.transpose(jnp.broadcast_to(row, (128, 128)))
    arrive(st)
    total = tsend[...]
    for d in range(1, 8):
        total = total + t_in[d - 1]
    tau_out[...] = total * (2.0 / (float(w_ref.shape[0] * 8) * float(w_ref.shape[1] * NX * NZ)))
    tau = tau_out[0:1, 0:1]

    def clip_rows(i, carry):
        sl = pl.ds(pl.multiple_of(i * 32, 32), 32)
        sc = scale_out[sl, 0:1]
        lim = tau / sc
        w = w_ref[sl, :].astype(F32)
        resid[sl, :] = jnp.clip(sc * w, -tau, tau).astype(BF16)
        rclip[sl, :] = jnp.clip(w, -lim, lim).astype(BF16)
        return carry

    lax.fori_loop(0, w_ref.shape[0] // 32, clip_rows, 0)
    arrive(g_z)
    g_z = h1z(4)
    arrive(g_h0z)
    g_h0z = h0z(2)

    nrow = w_ref.shape[0] // NX
    for i in range(NX):
        rp[i] = dot(resid[i * nrow:(i + 1) * nrow, :], sk_ref[...], 1, 0).astype(BF16)
    sx = [send(rp.at[xat(d)], rx_in.at[d - 1], dev(xx=xat(d))) for d in range(1, NX)]
    arrive(g_z)
    g_h1x = h1x1()
    arrive(sx)
    part = rp[x].astype(F32)
    for d in range(1, NX):
        part = part + rx_in[d - 1].astype(F32)
    rzs[...] = part.astype(BF16).reshape(NZ, nrow // NZ, RANK)
    sz = [send(rzs.at[zat(d)], rz_in.at[d - 1], dev(zz=zat(d))) for d in range(1, NZ)]
    arrive(g_h0z)
    g_h0z = h0z(3)
    arrive(sz)
    part = rzs[z].astype(F32)
    for d in range(1, NZ):
        part = part + rz_in[d - 1].astype(F32)
    rng[x, z] = part.astype(BF16)
    sz = [send(rng.at[x, z], rng.at[x, z], dev(zz=zat(d))) for d in range(1, NZ)]
    arrive(sz)
    sx = [send(rng.at[x], rng.at[x], dev(xx=xat(d))) for d in range(1, NX)]
    arrive(g_h1x)
    g_h1x = h1x2()
    arrive(g_h0z)
    g_h0z = h0z(4)
    arrive(sx)

    def whole_range():
        return rng[...].reshape(w_ref.shape[0], RANK)

    def scatter_core(part_ref, core_ref):
        return [send(part_ref.at[sib], core_ref, dev(kk=sib))]

    def scatter_y(part_ref, core_ref, sum_ref, in_ref, kind):
        sum_ref[...] = (part_ref[k].astype(F32) + core_ref[...].astype(F32)).astype(kind)
        return [send(sum_ref.at[yat(d)], in_ref.at[d - 1], dev(yy=yat(d))) for d in range(1, NY)]

    def owned(sum_ref, in_ref):
        out = sum_ref[y].astype(F32)
        for d in range(1, NY):
            out = out + in_ref[d - 1].astype(F32)
        return out

    whole = whole_range()
    gp[...] = dot(whole, whole, 0, 0).reshape(gp.shape)
    s_g = scatter_core(gp, gcore)
    zp[...] = dot(whole, resid[...], 0, 0).astype(BF16).reshape(zp.shape)
    arrive(s_g)
    s_g = scatter_y(gp, gcore, gs, gy_in, F32)
    s_z = scatter_core(zp, zcore)
    for i in range(8):
        sl = slice(128 * i, 128 * i + 128)
        inv = 1.0 / scale_out[sl, 0:1]
        rscaled[sl, :] = (rng[i // 2, 4 * (i % 2):4 * (i % 2) + 4].reshape(128, RANK).astype(F32) * inv).astype(BF16)
    arrive(s_g)
    gfull[k, y] = owned(gs, gy_in)
    s_g = [send(gfull.at[k, y], gfull.at[k, y], dev(yy=yat(d))) for d in range(1, NY)]
    arrive(s_z)
    s_z = scatter_y(zp, zcore, zs, zy_in, BF16)
    arrive(s_g)
    s_g = [send(gfull.at[k], gfull.at[k], dev(kk=sib))]
    arrive(s_z)
    z_out[k, y] = owned(zs, zy_in).astype(BF16)
    s_z = [send(z_out.at[k, y], z_out.at[k, y], dev(yy=yat(d))) for d in range(1, NY)]
    arrive(g_h0z)
    arrive(g_h1x)
    arrive(s_g)

    def tokens(yy, kk):
        return cal[yy, pl.ds(kk * 4, 4)].reshape(256, w_ref.shape[0])

    for yy in range(NY):
        block = tokens(yy, sib)
        ap[sib, yy] = dot(block, rclip[...], 1, 0).astype(BF16)
        qp[sib, yy] = dot(block, rscaled[...], 1, 0).astype(BF16)
    s_a, s_q = scatter_core(ap, acore), scatter_core(qp, qcore)
    for yy in range(NY):
        block = tokens(yy, k)
        ap[k, yy] = dot(block, rclip[...], 1, 0).astype(BF16)
        qp[k, yy] = dot(block, rscaled[...], 1, 0).astype(BF16)
    arrive(s_z)
    s_z = [send(z_out.at[k], z_out.at[k], dev(kk=sib))]
    arrive(s_a)
    s_a = scatter_y(ap, acore, asum, ay_in, BF16)
    arrive(s_q)
    s_q = scatter_y(qp, qcore, qs, qy_in, BF16)

    m_ref[:, :RANK] = gfull[...].reshape(RANK, RANK)
    ii = lax.broadcasted_iota(jnp.int32, (RANK, RANK), 0)
    jj = lax.broadcasted_iota(jnp.int32, (RANK, RANK), 1)
    m_ref[:, RANK:] = jnp.where(ii == jj, 1.0, 0.0)
    inverse_factor(m_ref, linv_out)

    arrive(s_z)
    arrive(s_q)
    q_out[...] = owned(qs, qy_in)
    arrive(s_a)
    a_out[...] = owned(asum, ay_in)
    for copy in pending:
        copy.wait_send()


def output_kernel(w_ref, a_ref, q_ref, linv_ref, rng_ref, z_ref, scale_ref, tau_ref, sparse_ref, basis_ref, coeffs_ref, err_ref):
    hi, lo = split2(linv_ref[...])
    pair = jnp.concatenate([hi, lo], axis=1)
    rng = rng_ref[...]
    basis_ref[...] = dot(jnp.concatenate([rng, rng], axis=1), pair, 1, 1).astype(BF16)
    zz = z_ref[...]
    coeffs = dot(pair, jnp.concatenate([zz, zz], axis=0), 1, 0).astype(BF16)
    coeffs_ref[...] = coeffs
    qh, ql = split2(q_ref[...])
    m = dot(jnp.concatenate([qh, qh, ql], axis=1), jnp.concatenate([hi, lo, hi], axis=1), 1, 1)
    mh, ml = split2(m)
    err_ref[...] = a_ref[...] - dot(jnp.concatenate([mh, ml], axis=1), jnp.concatenate([coeffs, coeffs], axis=0), 1, 0)
    tau = tau_ref[0:1, 0:1]

    def rows(i, carry):
        sl = pl.ds(pl.multiple_of(i * 32, 32), 32)
        scaled = scale_ref[sl, 0:1] * w_ref[sl, :].astype(F32)
        sparse_ref[sl, :] = (scaled - jnp.clip(scaled, -tau, tau)).astype(BF16)
        return carry

    lax.fori_loop(0, w_ref.shape[0] // 32, rows, 0)


def shards(weight, calib, sketch):
    d, f = weight.shape
    t = calib.shape[0]
    nrow = d // NX
    vm = pltpu.VMEM
    shape = jax.ShapeDtypeStruct
    out_shape = (
        shape((256, f), F32), shape((256, RANK), F32), shape((RANK, RANK), F32), shape((NX, NZ, nrow // NZ, RANK), BF16),
        shape((2, NY, 32, f), BF16), shape((d, 128), F32), shape((8, 128), F32),
    )
    scratch = [
        vm((NX, NZ, t, d), BF16),
        vm((2, d), F32), vm((NX - 1, 2, d), F32), vm((2, d), F32), vm((NZ - 1, 2, d), F32),
        vm((8, 128), F32), vm((7, 8, 128), F32),
        vm((d, f), BF16), vm((d, f), BF16),
        vm((NX, nrow, RANK), BF16), vm((NX - 1, nrow, RANK), BF16),
        vm((NZ, nrow // NZ, RANK), BF16), vm((NZ - 1, nrow // NZ, RANK), BF16),
    ]
    for kind, n, width in ((F32, 32, RANK),):
        scratch += [vm((2, NY, n, width), kind), vm((NY, n, width), kind), vm((NY, n, width), kind), vm((NY - 1, n, width), kind)]
    scratch += [vm((8, 128), F32), vm((2, NY, 32, RANK), F32)]
    for n, width in ((32, f), (256, RANK), (256, f)):
        scratch += [vm((2, NY, n, width), BF16), vm((NY, n, width), BF16), vm((NY, n, width), BF16), vm((NY - 1, n, width), BF16)]
    scratch += [vm((RANK, 2 * RANK), F32), vm((d, RANK), BF16)]
    scratch += [pltpu.SemaphoreType.DMA((128,)), pltpu.SemaphoreType.DMA((128,))]
    whole = pl.BlockSpec(memory_space=vm)
    a, q, linv, rng, zz, scale, tau = pl.pallas_call(
        exchange_kernel,
        out_shape=out_shape,
        in_specs=[whole] * 3,
        out_specs=[whole] * len(out_shape),
        scratch_shapes=scratch,
        compiler_params=pltpu.CompilerParams(collective_id=0, has_side_effects=True, vmem_limit_bytes=60 * 2**20),
    )(weight, calib, sketch)
    return pl.pallas_call(
        output_kernel,
        out_shape=(shape((d, f), BF16), shape((d, RANK), BF16), shape((RANK, f), BF16), shape((256, f), F32)),
        in_specs=[whole] * 8,
        out_specs=[whole] * 4,
        compiler_params=pltpu.CompilerParams(vmem_limit_bytes=60 * 2**20),
    )(weight, a, q, linv, rng.reshape(d, RANK), zz.reshape(RANK, f), scale, tau)


def solution(mesh):
    return jax.shard_map(
        shards,
        mesh=mesh,
        in_specs=(P("cols", "rows"), P("rows", "cols"), P("rows", None)),
        out_specs=(P("cols", "rows"), P("cols", None), P(None, "rows"), P("cols", "rows")),
        check_vma=False,
    )
```

```python
import jax
import jax.numpy as jnp
from jax import lax
from jax.experimental import pallas as pl
from jax.experimental.pallas import tpu as pltpu
from jax.sharding import PartitionSpec as P

MESH = pl.DeviceIdType.MESH
F32, BF16 = jnp.float32, jnp.bfloat16
NX, NZ, NY = 4, 8, 4
RANK = 256
PANEL = 32
CUT = 32


def split3(v):
    a = v.astype(BF16)
    rest = v - a.astype(F32)
    b = rest.astype(BF16)
    return a, b, (rest - b.astype(F32)).astype(BF16)


def split2(v):
    a = v.astype(BF16)
    return a, (v - a.astype(F32)).astype(BF16)


def dot(a, b, ca, cb):
    return lax.dot_general(a, b, (((ca,), (cb,)), ((), ())), preferred_element_type=F32)


def inverse_factor(m_ref, out_ref):
    lane = lax.broadcasted_iota(jnp.int32, (PANEL, 2 * RANK), 1)
    sub8 = lax.broadcasted_iota(jnp.int32, (8, 128), 0)
    groups = PANEL // 8

    def panel(step, carry):
        k0 = pl.multiple_of(step * PANEL, PANEL)
        rows = m_ref[pl.ds(k0, PANEL), :]
        rows = jnp.where(lane >= k0, rows, 0.0)
        diag = pltpu.roll(rows[:, :RANK], lax.rem(RANK - k0, RANK), 1)[:, :128]
        rg = [rows[8 * g:8 * g + 8, :] for g in range(groups)]
        dg = [diag[8 * g:8 * g + 8, :] for g in range(groups)]
        for q in range(groups):
            left = range(groups - q)
            col = [
                [jnp.broadcast_to(dg[g][:, 8 * q + j:8 * q + j + 1], (8, 128)) for g in range(q, groups)]
                for j in range(8)
            ]
            pivots = jnp.zeros((8, 128), F32)
            for j in range(8):
                pivot = jnp.broadcast_to(col[j][0][j:j + 1, :], (8, 128))
                inv = 1.0 / pivot
                pivots = jnp.where(sub8 == j, pivot, pivots)
                mult = [col[j][g] * inv for g in left]
                mult[0] = jnp.where(sub8 > j, mult[0], 0.0)
                for other in range(j + 1, 8):
                    row = jnp.broadcast_to(col[other][0][j:j + 1, :], (8, 128))
                    for g in left:
                        col[other][g] = col[other][g] - mult[g] * row
                rrow, drow = rg[q][j:j + 1, :], dg[q][j:j + 1, :]
                for g in left:
                    rg[q + g] = rg[q + g] - jnp.concatenate([mult[g]] * 4, axis=1) * rrow
                    dg[q + g] = dg[q + g] - mult[g] * drow
            root = lax.rsqrt(pivots)
            rg[q] = rg[q] * jnp.concatenate([root] * 4, axis=1)
        done = jnp.concatenate(rg, axis=0)
        out_ref[pl.ds(k0, PANEL), :] = done[:, RANK:]
        a, b, c = split3(done)
        lhs = jnp.concatenate([a, a, b, a, b, c], axis=0)[:, :RANK]
        rhs = jnp.concatenate([a, b, a, c, b, a], axis=0)
        m_ref[...] -= dot(lhs, rhs, 0, 0)
        return carry

    lax.fori_loop(0, RANK // PANEL, panel, 0)


def exchange_kernel(
    w_in, cal_in, sk_in,
    a_out, q_out, linv_out, rng_out, z_out, scale_out, tau_out,
    w_ref, sk_ref, cal, stx, stx_in, stz, stz_in, tsend, t_in, tau_ref, scale, resid, rclip, rp, rx_in, rzs, rz_in, rng, rscaled,
    gp, gcore, gs, gy_in, gfull, zp, zcore, zs, zy_in, zfull, qp, qcore, qs, qy_in, qsum, ap, acore, asum, ay1, ay2, atot, m_ref, linv,
    ssem, rsem, lsem,
):
    rr, cc = lax.axis_index("rows"), lax.axis_index("cols")
    x, z = rr // NZ, lax.rem(rr, NZ)
    y, k = cc // 2, lax.rem(cc, 2)
    sib = 1 - k
    rows_d, cols_f = w_ref.shape

    def xat(d):
        return lax.rem(x + d, NX)

    def zat(d):
        return lax.rem(z + d, NZ)

    def yat(d):
        return lax.rem(y + d, NY)

    def dev(xx=x, zz=z, yy=y, kk=k):
        return (xx * NZ + zz, yy * 2 + kk)

    used = [0, 0]
    pending, stores = [], []

    def send(src, dst, to):
        i = used[0]
        used[0] += 1
        copy = pltpu.make_async_remote_copy(
            src_ref=src, dst_ref=dst, send_sem=ssem.at[i], recv_sem=rsem.at[i], device_id=to, device_id_type=MESH
        )
        copy.start()
        pending.append(copy)
        return copy

    def arrive(copies):
        for copy in copies:
            copy.wait_recv()

    def local(src, dst):
        i = used[1]
        used[1] += 1
        copy = pltpu.make_async_copy(src, dst, lsem.at[i])
        copy.start()
        return copy

    def store(src, dst):
        stores.append(local(src, dst))

    load_cal = local(cal_in, cal.at[x, z])
    load_w = local(w_in, w_ref)
    load_sk = local(sk_in, sk_ref)

    barrier = pltpu.get_barrier_semaphore()
    partners = [dev(xx=xat(d)) for d in range(1, NX)] + [dev(zz=zat(d)) for d in range(1, NZ)]
    partners += [(rr, lax.rem(cc + d, 8)) for d in range(1, 8)]
    for p in partners:
        pl.semaphore_signal(barrier, inc=1, device_id=p, device_id_type=MESH)

    load_cal.wait()
    for i in range(2):
        part = cal[x, z, :, 512 * i:512 * i + 512].astype(F32)
        stx[0:1, 512 * i:512 * i + 512] = jnp.sum(part * part, axis=0, keepdims=True)
    load_w.wait()
    ones = jnp.ones((8, cols_f), BF16)
    for i in range(4):
        stx[1:2, 256 * i:256 * i + 256] = dot(ones, jnp.abs(w_ref[256 * i:256 * i + 256, :]), 1, 1)[0:1, :]
    pl.semaphore_wait(barrier, len(partners))

    xp, xm, zp_, zm = xat(1), xat(NX - 1), zat(1), zat(NZ - 1)
    half = rows_d // 2
    lower, upper = pl.ds(0, half), pl.ds(half, half)
    first, second = pl.ds(0, CUT), pl.ds(CUT, 64 - CUT)

    def both(up, down, along):
        if along == 0:
            return [send(up, up, dev(xx=xp)), send(down, down, dev(xx=xm))]
        return [send(up, up, dev(zz=zp_)), send(down, down, dev(zz=zm))]

    def lane_first():
        copies = both(cal.at[x, z, first], cal.at[x, z, first], 0)
        yield
        arrive(copies)
        copies = both(cal.at[xm, z, first, lower], cal.at[xp, z, first, upper], 0)
        yield
        arrive(copies)
        for step in range(1, 5):
            part = (slice(None),) * 2 if step < 4 else (lower, upper)
            copies = both(cal.at[:, zat(NZ - step + 1), first, part[0]], cal.at[:, zat(step - 1), first, part[1]], 1)
            yield
            arrive(copies)
        yield

    def lane_second():
        for step in range(1, 5):
            part = (slice(None),) * 2 if step < 4 else (lower, upper)
            copies = both(cal.at[x, zat(NZ - step + 1), second, part[0]], cal.at[x, zat(step - 1), second, part[1]], 1)
            yield
            arrive(copies)
        copies = both(cal.at[x, :, second], cal.at[x, :, second], 0)
        yield
        arrive(copies)
        copies = both(cal.at[xm, :, second, lower], cal.at[xp, :, second, upper], 0)
        yield
        arrive(copies)
        yield

    lane1, lane2 = lane_first(), lane_second()

    sx = [send(stx, stx_in.at[d - 1], dev(xx=xat(d))) for d in range(1, NX)]
    next(lane1)
    next(lane2)
    arrive(sx)
    stz[...] = stx[...] + stx_in[0] + stx_in[1] + stx_in[2]
    sz = [send(stz, stz_in.at[d - 1], dev(zz=zat(d))) for d in range(1, NZ)]
    next(lane1)
    next(lane2)
    arrive(sz)
    tot = stz[...]
    for d in range(1, NZ):
        tot = tot + stz_in[d - 1]
    scale_row = jnp.sqrt(tot[0:1, :] / (NX * NZ * cal_in.shape[0]) + 1e-06)
    mine = jnp.sum(scale_row * tot[1:2, :], axis=1, keepdims=True)
    tsend[...] = jnp.broadcast_to(mine, (8, 128))
    st = [send(tsend, t_in.at[d - 1], (rr, lax.rem(cc + d, 8))) for d in range(1, 8)]
    next(lane1)
    next(lane2)
    for i in range(8):
        row = scale_row[:, 128 * i:128 * i + 128]
        scale[128 * i:128 * i + 128, :] = jnp.transpose(jnp.broadcast_to(row, (128, 128)))
    store(scale, scale_out)
    arrive(st)
    total = tsend[...]
    for d in range(1, 8):
        total = total + t_in[d - 1]
    tau_ref[...] = total * (2.0 / (float(rows_d * 8) * float(cols_f * NX * NZ)))
    store(tau_ref, tau_out)
    tau = tau_ref[0:1, 0:1]

    def clip_rows(i, carry):
        sl = pl.ds(pl.multiple_of(i * 32, 32), 32)
        sc = scale[sl, 0:1]
        lim = tau / sc
        w = w_ref[sl, :].astype(F32)
        resid[sl, :] = jnp.clip(sc * w, -tau, tau).astype(BF16)
        rclip[sl, :] = jnp.clip(w, -lim, lim).astype(BF16)
        return carry

    next(lane2)
    lax.fori_loop(0, rows_d // 32, clip_rows, 0)

    nrow = rows_d // NX
    load_sk.wait()
    sx = []
    for d in (2, 1, 3, 0):
        i = xat(d)
        rp[i] = dot(resid[pl.ds(pl.multiple_of(i * nrow, nrow), nrow), :], sk_ref[...], 1, 0).astype(BF16)
        if d:
            sx.append(send(rp.at[i], rx_in.at[d - 1], dev(xx=i)))
    next(lane1)
    next(lane2)
    arrive(sx)
    part = rp[x].astype(F32)
    for d in range(1, NX):
        part = part + rx_in[d - 1].astype(F32)
    rzs[...] = part.astype(BF16).reshape(NZ, nrow // NZ, RANK)
    sz = [send(rzs.at[zat(d)], rz_in.at[d - 1], dev(zz=zat(d))) for d in range(1, NZ)]
    next(lane1)
    arrive(sz)
    part = rzs[z].astype(F32)
    for d in range(1, NZ):
        part = part + rz_in[d - 1].astype(F32)
    rng[x, z] = part.astype(BF16)
    sz = [send(rng.at[x, z], rng.at[x, z], dev(zz=zat(d))) for d in range(1, NZ)]
    next(lane1)
    next(lane2)

    def scatter_core(part_ref, core_ref):
        return [send(part_ref.at[sib], core_ref, dev(kk=sib))]

    def lane_products(b, tokens, n):
        def fill(kk):
            for yy in range(NY):
                block = cal[yy, pl.ds(kk * 4, 4), tokens].reshape(4 * n, rows_d)
                ap[b][kk, yy] = dot(block, rclip[...], 1, 0).astype(BF16)

        fill(sib)
        copies = scatter_core(ap[b], acore[b])
        fill(k)
        yield
        arrive(copies)
        for yy in range(NY):
            asum[b][yy] = (ap[b][k, yy].astype(F32) + acore[b][yy].astype(F32)).astype(BF16)
        lo, hi = pl.ds(0, 2 * n), pl.ds(2 * n, 2 * n)
        yp, ym = yat(1), yat(NY - 1)
        copies = [send(asum[b].at[yat(2), lo], ay1[b].at[0], dev(yy=yp)), send(asum[b].at[yat(2), hi], ay1[b].at[1], dev(yy=ym))]
        yield
        arrive(copies)
        asum[b][yp, lo] = (asum[b][yp, lo].astype(F32) + ay1[b][0].astype(F32)).astype(BF16)
        asum[b][ym, hi] = (asum[b][ym, hi].astype(F32) + ay1[b][1].astype(F32)).astype(BF16)
        copies = [send(asum[b].at[yp], ay2[b].at[0], dev(yy=yp)), send(asum[b].at[ym], ay2[b].at[1], dev(yy=ym))]
        yield
        arrive(copies)
        whole = asum[b][y].astype(F32) + ay2[b][0].astype(F32) + ay2[b][1].astype(F32)
        atot[:, tokens, :] = whole.reshape(4, n, cols_f)
        yield

    batch1, batch2 = lane_products(0, first, CUT), lane_products(1, second, 64 - CUT)

    arrive(sz)
    sx = [send(rng.at[x], rng.at[x], dev(xx=xat(d))) for d in range(1, NX)]
    next(lane1)
    next(batch1)
    next(batch1)
    next(lane2)
    next(batch2)
    next(batch1)
    arrive(sx)
    store(rng, rng_out)

    def scatter_y(part_ref, core_ref, sum_ref, in_ref, kind):
        sum_ref[...] = (part_ref[k].astype(F32) + core_ref[...].astype(F32)).astype(kind)
        return [send(sum_ref.at[yat(d)], in_ref.at[d - 1], dev(yy=yat(d))) for d in range(1, NY)]

    def owned(sum_ref, in_ref):
        out = sum_ref[y].astype(F32)
        for d in range(1, NY):
            out = out + in_ref[d - 1].astype(F32)
        return out

    whole = rng[...].reshape(rows_d, RANK)
    gp[...] = dot(whole, whole, 0, 0).reshape(gp.shape)
    s_g = scatter_core(gp, gcore)
    zp[...] = dot(whole, resid[...], 0, 0).astype(BF16).reshape(zp.shape)
    arrive(s_g)
    s_g = scatter_y(gp, gcore, gs, gy_in, F32)
    next(batch2)
    s_z = scatter_core(zp, zcore)
    for i in range(8):
        sl = slice(128 * i, 128 * i + 128)
        inv = 1.0 / scale[sl, 0:1]
        rscaled[sl, :] = (rng[i // 2, 4 * (i % 2):4 * (i % 2) + 4].reshape(128, RANK).astype(F32) * inv).astype(BF16)
    arrive(s_g)
    gfull[k, y] = owned(gs, gy_in)
    s_g = [send(gfull.at[k, y], gfull.at[k, y], dev(yy=yat(d))) for d in range(1, NY)]
    next(batch2)
    arrive(s_z)
    s_z = scatter_y(zp, zcore, zs, zy_in, BF16)
    for yy in range(NY):
        qp[sib, yy] = dot(cal[yy, pl.ds(sib * 4, 4)].reshape(256, rows_d), rscaled[...], 1, 0).astype(BF16)
    s_q = scatter_core(qp, qcore)
    for yy in range(NY):
        qp[k, yy] = dot(cal[yy, pl.ds(k * 4, 4)].reshape(256, rows_d), rscaled[...], 1, 0).astype(BF16)
    arrive(s_g)
    s_g = [send(gfull.at[k], gfull.at[k], dev(kk=sib))]
    arrive(s_q)
    s_q = scatter_y(qp, qcore, qs, qy_in, BF16)
    arrive(s_z)
    zfull[k, y] = owned(zs, zy_in).astype(BF16)
    s_z = [send(zfull.at[k, y], zfull.at[k, y], dev(yy=yat(d))) for d in range(1, NY)]
    arrive(s_g)

    m_ref[:, :RANK] = gfull[...].reshape(RANK, RANK)
    ii = lax.broadcasted_iota(jnp.int32, (RANK, RANK), 0)
    jj = lax.broadcasted_iota(jnp.int32, (RANK, RANK), 1)
    m_ref[:, RANK:] = jnp.where(ii == jj, 1.0, 0.0)
    inverse_factor(m_ref, linv)
    store(linv, linv_out)

    arrive(s_z)
    s_z = [send(zfull.at[k], zfull.at[k], dev(kk=sib))]
    next(batch1)
    next(batch2)
    store(atot, a_out)
    arrive(s_q)
    qsum[...] = owned(qs, qy_in)
    store(qsum, q_out)
    arrive(s_z)
    store(zfull, z_out)
    for copy in pending:
        copy.wait_send()
    for copy in stores:
        copy.wait()


def output_kernel(
    w_in, a_in, q_in, linv_in, rng_in, z_in, scale_in, tau_in, sparse_out, basis_out, coeffs_out, err_out,
    w_ref, a_ref, q_ref, linv_ref, rng_ref, z_ref, scale_ref, tau_ref, sparse_ref, basis_ref, coeffs_ref, err_ref, lsem,
):
    used = [0]

    def copy(src, dst):
        i = used[0]
        used[0] += 1
        out = pltpu.make_async_copy(src, dst, lsem.at[i])
        out.start()
        return out

    parts = 4
    n = w_ref.shape[0] // parts
    cut = [pl.ds(i * n, n) for i in range(parts)]
    small = [copy(tau_in, tau_ref), copy(scale_in, scale_ref)]
    loads_w = [copy(w_in.at[c], w_ref.at[c]) for c in cut]
    loads_b = [copy(linv_in, linv_ref), copy(rng_in, rng_ref)]
    load_z, load_q, load_a = copy(z_in, z_ref), copy(q_in, q_ref), copy(a_in, a_ref)
    for c in small:
        c.wait()
    tau = tau_ref[0:1, 0:1]
    stores = []
    for p in range(parts):
        loads_w[p].wait()

        def rows(i, carry, p=p):
            sl = pl.ds(pl.multiple_of(p * n + i * 32, 32), 32)
            scaled = scale_ref[sl, 0:1] * w_ref[sl, :].astype(F32)
            sparse_ref[sl, :] = (scaled - jnp.clip(scaled, -tau, tau)).astype(BF16)
            return carry

        lax.fori_loop(0, n // 32, rows, 0)
        stores.append(copy(sparse_ref.at[cut[p]], sparse_out.at[cut[p]]))
    for c in loads_b:
        c.wait()
    hi, lo = split2(linv_ref[...])
    pair = jnp.concatenate([hi, lo], axis=1)
    rng = rng_ref[...]
    basis_ref[...] = dot(jnp.concatenate([rng, rng], axis=1), pair, 1, 1).astype(BF16)
    stores.append(copy(basis_ref, basis_out))
    load_z.wait()
    zz = z_ref[...]
    coeffs = dot(pair, jnp.concatenate([zz, zz], axis=0), 1, 0).astype(BF16)
    coeffs_ref[...] = coeffs
    stores.append(copy(coeffs_ref, coeffs_out))
    load_q.wait()
    qh, ql = split2(q_ref[...])
    m = dot(jnp.concatenate([qh, qh, ql], axis=1), jnp.concatenate([hi, lo, hi], axis=1), 1, 1)
    mh, ml = split2(m)
    load_a.wait()
    err_ref[...] = a_ref[...] - dot(jnp.concatenate([mh, ml], axis=1), jnp.concatenate([coeffs, coeffs], axis=0), 1, 0)
    stores.append(copy(err_ref, err_out))
    for c in stores:
        c.wait()


def shards(weight, calib, sketch):
    d, f = weight.shape
    t = calib.shape[0]
    nrow = d // NX
    vm = pltpu.VMEM
    shape = jax.ShapeDtypeStruct
    out_shape = (
        shape((4, t, f), F32), shape((256, RANK), F32), shape((RANK, RANK), F32), shape((NX, NZ, nrow // NZ, RANK), BF16),
        shape((2, NY, 32, f), BF16), shape((d, 128), F32), shape((8, 128), F32),
    )

    def scatter(n, width, kind):
        return [vm((2, NY, n, width), kind), vm((NY, n, width), kind), vm((NY, n, width), kind), vm((NY - 1, n, width), kind)]

    batches = (CUT, t - CUT)
    scratch = [
        vm((d, f), BF16), vm((f, RANK), BF16), vm((NX, NZ, t, d), BF16),
        vm((2, d), F32), vm((NX - 1, 2, d), F32), vm((2, d), F32), vm((NZ - 1, 2, d), F32),
        vm((8, 128), F32), vm((7, 8, 128), F32), vm((8, 128), F32), vm((d, 128), F32),
        vm((d, f), BF16), vm((d, f), BF16),
        vm((NX, nrow, RANK), BF16), vm((NX - 1, nrow, RANK), BF16),
        vm((NZ, nrow // NZ, RANK), BF16), vm((NZ - 1, nrow // NZ, RANK), BF16),
        vm((NX, NZ, nrow // NZ, RANK), BF16), vm((d, RANK), BF16),
        *scatter(32, RANK, F32), vm((2, NY, 32, RANK), F32),
        *scatter(32, f, BF16), vm((2, NY, 32, f), BF16),
        *scatter(256, RANK, BF16), vm((256, RANK), F32),
        [vm((2, NY, 4 * n, f), BF16) for n in batches],
        [vm((NY, 4 * n, f), BF16) for n in batches],
        [vm((NY, 4 * n, f), BF16) for n in batches],
        [vm((2, 2 * n, f), BF16) for n in batches],
        [vm((2, 4 * n, f), BF16) for n in batches],
        vm((4, t, f), F32), vm((RANK, 2 * RANK), F32), vm((RANK, RANK), F32),
        pltpu.SemaphoreType.DMA((128,)), pltpu.SemaphoreType.DMA((128,)), pltpu.SemaphoreType.DMA((16,)),
    ]
    anywhere = pl.BlockSpec(memory_space=pl.ANY)
    a, q, linv, rng, zz, scale, tau = pl.pallas_call(
        exchange_kernel,
        out_shape=out_shape,
        in_specs=[anywhere] * 3,
        out_specs=[anywhere] * len(out_shape),
        scratch_shapes=scratch,
        compiler_params=pltpu.CompilerParams(collective_id=0, has_side_effects=True, vmem_limit_bytes=60 * 2**20),
    )(weight, calib, sketch)
    ins = (weight, a.reshape(256, f), q, linv, rng.reshape(d, RANK), zz.reshape(RANK, f), scale, tau)
    out_shape = (shape((d, f), BF16), shape((d, RANK), BF16), shape((RANK, f), BF16), shape((256, f), F32))
    return pl.pallas_call(
        output_kernel,
        out_shape=out_shape,
        in_specs=[anywhere] * 8,
        out_specs=[anywhere] * 4,
        scratch_shapes=[vm(v.shape, v.dtype) for v in (*ins, *out_shape)] + [pltpu.SemaphoreType.DMA((24,))],
        compiler_params=pltpu.CompilerParams(vmem_limit_bytes=60 * 2**20),
    )(*ins)


def solution(mesh):
    return jax.shard_map(
        shards,
        mesh=mesh,
        in_specs=(P("cols", "rows"), P("rows", "cols"), P("rows", None)),
        out_specs=(P("cols", "rows"), P("cols", None), P(None, "rows"), P("cols", "rows")),
        check_vma=False,
    )
```

```python
import jax
import jax.numpy as jnp
from jax import lax
from jax.experimental import pallas as pl
from jax.experimental.pallas import tpu as pltpu
from jax.sharding import PartitionSpec as P

MESH = pl.DeviceIdType.MESH
F32, BF16 = jnp.float32, jnp.bfloat16
NX, NZ, NY = 4, 8, 4
RANK = 256
PANEL = 32
CUT = 32


def split3(v):
    a = v.astype(BF16)
    rest = v - a.astype(F32)
    b = rest.astype(BF16)
    return a, b, (rest - b.astype(F32)).astype(BF16)


def split2(v):
    a = v.astype(BF16)
    return a, (v - a.astype(F32)).astype(BF16)


def dot(a, b, ca, cb):
    return lax.dot_general(a, b, (((ca,), (cb,)), ((), ())), preferred_element_type=F32)


def inverse_factor(m_ref, out_ref, start, stop):
    lane = lax.broadcasted_iota(jnp.int32, (PANEL, 2 * RANK), 1)
    sub8 = lax.broadcasted_iota(jnp.int32, (8, 128), 0)
    groups = PANEL // 8

    def panel(step, carry):
        k0 = pl.multiple_of(step * PANEL, PANEL)
        rows = m_ref[pl.ds(k0, PANEL), :]
        rows = jnp.where(lane >= k0, rows, 0.0)
        diag = pltpu.roll(rows[:, :RANK], lax.rem(RANK - k0, RANK), 1)[:, :128]
        rg = [rows[8 * g:8 * g + 8, :] for g in range(groups)]
        dg = [diag[8 * g:8 * g + 8, :] for g in range(groups)]
        for q in range(groups):
            left = range(groups - q)
            col = [
                [jnp.broadcast_to(dg[g][:, 8 * q + j:8 * q + j + 1], (8, 128)) for g in range(q, groups)]
                for j in range(8)
            ]
            pivots = jnp.zeros((8, 128), F32)
            for j in range(8):
                pivot = jnp.broadcast_to(col[j][0][j:j + 1, :], (8, 128))
                inv = 1.0 / pivot
                pivots = jnp.where(sub8 == j, pivot, pivots)
                mult = [col[j][g] * inv for g in left]
                mult[0] = jnp.where(sub8 > j, mult[0], 0.0)
                for other in range(j + 1, 8):
                    row = jnp.broadcast_to(col[other][0][j:j + 1, :], (8, 128))
                    for g in left:
                        col[other][g] = col[other][g] - mult[g] * row
                rrow, drow = rg[q][j:j + 1, :], dg[q][j:j + 1, :]
                for g in left:
                    rg[q + g] = rg[q + g] - jnp.concatenate([mult[g]] * 4, axis=1) * rrow
                    dg[q + g] = dg[q + g] - mult[g] * drow
            root = lax.rsqrt(pivots)
            rg[q] = rg[q] * jnp.concatenate([root] * 4, axis=1)
        done = jnp.concatenate(rg, axis=0)
        out_ref[pl.ds(k0, PANEL), :] = done[:, RANK:]
        a, b, c = split3(done)
        lhs = jnp.concatenate([a, a, b, a, b, c], axis=0)[:, :RANK]
        rhs = jnp.concatenate([a, b, a, c, b, a], axis=0)
        m_ref[...] -= dot(lhs, rhs, 0, 0)
        return carry

    lax.fori_loop(start, stop, panel, 0)


def exchange_kernel(
    w_in, cal_in, sk_in,
    a_out, q_out, linv_out, rng_out, z_out, scale_out, tau_out,
    w_ref, sk_ref, cal, stx, stx_in, stz, stz_in, tsend, t_in, tau_ref, scale, resid, rclip, rp, rx_in, rzs, rz_in, rng, rscaled,
    gp, gcore, gs, gy_in, gfull, zp, zcore, zs, zy_in, zfull, qp, qcore, qs, qy_in, qfull, ap, acore, asum, ay1, ay2, atot, m_ref, linv,
    ssem, rsem, lsem,
):
    rr, cc = lax.axis_index("rows"), lax.axis_index("cols")
    x, z = rr // NZ, lax.rem(rr, NZ)
    y, k = cc // 2, lax.rem(cc, 2)
    sib = 1 - k
    rows_d, cols_f = w_ref.shape

    def xat(d):
        return lax.rem(x + d, NX)

    def zat(d):
        return lax.rem(z + d, NZ)

    def yat(d):
        return lax.rem(y + d, NY)

    def dev(xx=x, zz=z, yy=y, kk=k):
        return (xx * NZ + zz, yy * 2 + kk)

    used = [0, 0]
    pending, stores = [], []

    def send(src, dst, to):
        i = used[0]
        used[0] += 1
        copy = pltpu.make_async_remote_copy(
            src_ref=src, dst_ref=dst, send_sem=ssem.at[i], recv_sem=rsem.at[i], device_id=to, device_id_type=MESH
        )
        copy.start()
        pending.append(copy)
        return copy

    def arrive(copies):
        for copy in copies:
            copy.wait_recv()

    def local(src, dst):
        i = used[1]
        used[1] += 1
        copy = pltpu.make_async_copy(src, dst, lsem.at[i])
        copy.start()
        return copy

    def store(src, dst):
        stores.append(local(src, dst))

    load_cal = local(cal_in, cal.at[x, z])
    load_w = local(w_in, w_ref)
    load_sk = local(sk_in, sk_ref)

    barrier = pltpu.get_barrier_semaphore()
    partners = [dev(xx=xat(d)) for d in range(1, NX)] + [dev(zz=zat(d)) for d in range(1, NZ)]
    partners += [(rr, lax.rem(cc + d, 8)) for d in range(1, 8)]
    for p in partners:
        pl.semaphore_signal(barrier, inc=1, device_id=p, device_id_type=MESH)

    load_cal.wait()
    for i in range(2):
        part = cal[x, z, :, 512 * i:512 * i + 512].astype(F32)
        stx[0:1, 512 * i:512 * i + 512] = jnp.sum(part * part, axis=0, keepdims=True)
    load_w.wait()
    ones = jnp.ones((8, cols_f), BF16)
    for i in range(4):
        stx[1:2, 256 * i:256 * i + 256] = dot(ones, jnp.abs(w_ref[256 * i:256 * i + 256, :]), 1, 1)[0:1, :]
    pl.semaphore_wait(barrier, len(partners))

    xp, xm, zp_, zm = xat(1), xat(NX - 1), zat(1), zat(NZ - 1)
    half = rows_d // 2
    lower, upper = pl.ds(0, half), pl.ds(half, half)
    first, second = pl.ds(0, CUT), pl.ds(CUT, 64 - CUT)

    def both(up, down, along):
        if along == 0:
            return [send(up, up, dev(xx=xp)), send(down, down, dev(xx=xm))]
        return [send(up, up, dev(zz=zp_)), send(down, down, dev(zz=zm))]

    def lane_first():
        copies = both(cal.at[x, z, first], cal.at[x, z, first], 0)
        yield
        arrive(copies)
        copies = both(cal.at[xm, z, first, lower], cal.at[xp, z, first, upper], 0)
        yield
        arrive(copies)
        for step in range(1, 5):
            part = (slice(None),) * 2 if step < 4 else (lower, upper)
            copies = both(cal.at[:, zat(NZ - step + 1), first, part[0]], cal.at[:, zat(step - 1), first, part[1]], 1)
            yield
            arrive(copies)
        yield

    def lane_second():
        for step in range(1, 5):
            part = (slice(None),) * 2 if step < 4 else (lower, upper)
            copies = both(cal.at[x, zat(NZ - step + 1), second, part[0]], cal.at[x, zat(step - 1), second, part[1]], 1)
            yield
            arrive(copies)
        copies = both(cal.at[x, :, second], cal.at[x, :, second], 0)
        yield
        arrive(copies)
        copies = both(cal.at[xm, :, second, lower], cal.at[xp, :, second, upper], 0)
        yield
        arrive(copies)
        yield

    lane1, lane2 = lane_first(), lane_second()

    sx = [send(stx, stx_in.at[d - 1], dev(xx=xat(d))) for d in range(1, NX)]
    next(lane1)
    next(lane2)
    arrive(sx)
    stz[...] = stx[...] + stx_in[0] + stx_in[1] + stx_in[2]
    sz = [send(stz, stz_in.at[d - 1], dev(zz=zat(d))) for d in range(1, NZ)]
    next(lane1)
    next(lane2)
    arrive(sz)
    tot = stz[...]
    for d in range(1, NZ):
        tot = tot + stz_in[d - 1]
    scale_row = jnp.sqrt(tot[0:1, :] / (NX * NZ * cal_in.shape[0]) + 1e-06)
    mine = jnp.sum(scale_row * tot[1:2, :], axis=1, keepdims=True)
    tsend[...] = jnp.broadcast_to(mine, (8, 128))
    st = [send(tsend, t_in.at[d - 1], (rr, lax.rem(cc + d, 8))) for d in range(1, 8)]
    next(lane1)
    next(lane2)
    for i in range(8):
        row = scale_row[:, 128 * i:128 * i + 128]
        scale[128 * i:128 * i + 128, :] = jnp.transpose(jnp.broadcast_to(row, (128, 128)))
    store(scale, scale_out)
    arrive(st)
    total = tsend[...]
    for d in range(1, 8):
        total = total + t_in[d - 1]
    tau_ref[...] = total * (2.0 / (float(rows_d * 8) * float(cols_f * NX * NZ)))
    store(tau_ref, tau_out)
    tau = tau_ref[0:1, 0:1]

    def clip_rows(i, carry):
        sl = pl.ds(pl.multiple_of(i * 32, 32), 32)
        sc = scale[sl, :]
        lim = tau / sc
        for t in range(cols_f // 128):
            tl = pl.ds(128 * t, 128)
            w = w_ref[sl, tl].astype(F32)
            resid[sl, tl] = jnp.clip(sc * w, -tau, tau).astype(BF16)
            rclip[sl, tl] = jnp.clip(w, -lim, lim).astype(BF16)
        return carry

    lax.fori_loop(0, rows_d // 64, clip_rows, 0)
    next(lane1)
    next(lane2)
    lax.fori_loop(rows_d // 64, rows_d // 32, clip_rows, 0)

    def scatter_core(part_ref, core_ref):
        return [send(part_ref.at[sib], core_ref, dev(kk=sib))]

    def lane_products(b, tokens, n):
        def fill(kk):
            for yy in range(NY):
                block = cal[yy, pl.ds(kk * 4, 4), tokens].reshape(4 * n, rows_d)
                ap[b][kk, yy] = dot(block, rclip[...], 1, 0).astype(BF16)

        fill(sib)
        copies = scatter_core(ap[b], acore[b])
        fill(k)
        yield
        arrive(copies)
        for yy in range(NY):
            asum[b][yy] = (ap[b][k, yy].astype(F32) + acore[b][yy].astype(F32)).astype(BF16)
        lo, hi = pl.ds(0, 2 * n), pl.ds(2 * n, 2 * n)
        yp, ym = yat(1), yat(NY - 1)
        copies = [send(asum[b].at[yat(2), lo], ay1[b].at[0], dev(yy=yp)), send(asum[b].at[yat(2), hi], ay1[b].at[1], dev(yy=ym))]
        yield
        arrive(copies)
        asum[b][yp, lo] = (asum[b][yp, lo].astype(F32) + ay1[b][0].astype(F32)).astype(BF16)
        asum[b][ym, hi] = (asum[b][ym, hi].astype(F32) + ay1[b][1].astype(F32)).astype(BF16)
        copies = [send(asum[b].at[yp], ay2[b].at[0], dev(yy=yp)), send(asum[b].at[ym], ay2[b].at[1], dev(yy=ym))]
        yield
        arrive(copies)
        whole = asum[b][y].astype(F32) + ay2[b][0].astype(F32) + ay2[b][1].astype(F32)
        atot[:, tokens, :] = whole.reshape(4, n, cols_f)
        yield

    batch1, batch2 = lane_products(0, first, CUT), lane_products(1, second, 64 - CUT)

    nrow = rows_d // NX
    load_sk.wait()
    sx = []
    for d in (2, 1, 3, 0):
        i = xat(d)
        rp[i] = dot(resid[pl.ds(pl.multiple_of(i * nrow, nrow), nrow), :], sk_ref[...], 1, 0).astype(BF16)
        if d:
            sx.append(send(rp.at[i], rx_in.at[d - 1], dev(xx=i)))
    next(lane1)
    next(lane2)
    arrive(sx)
    part = rp[x].astype(F32)
    for d in range(1, NX):
        part = part + rx_in[d - 1].astype(F32)
    rzs[...] = part.astype(BF16).reshape(NZ, nrow // NZ, RANK)
    sz = [send(rzs.at[zat(d)], rz_in.at[d - 1], dev(zz=zat(d))) for d in range(1, NZ)]
    next(lane1)
    arrive(sz)
    part = rzs[z].astype(F32)
    for d in range(1, NZ):
        part = part + rz_in[d - 1].astype(F32)
    rng[x, z] = part.astype(BF16)
    sz = [send(rng.at[x, z], rng.at[x, z], dev(zz=zat(d))) for d in range(1, NZ)]
    next(lane1)
    next(lane2)
    next(batch1)

    arrive(sz)
    sx = [send(rng.at[x], rng.at[x], dev(xx=xat(d))) for d in range(1, NX)]
    next(batch1)
    next(lane2)
    next(batch2)
    next(batch1)
    next(batch2)
    arrive(sx)
    store(rng, rng_out)

    def scatter_y(part_ref, core_ref, sum_ref, in_ref, kind):
        sum_ref[...] = (part_ref[k].astype(F32) + core_ref[...].astype(F32)).astype(kind)
        return [send(sum_ref.at[yat(d)], in_ref.at[d - 1], dev(yy=yat(d))) for d in range(1, NY)]

    def owned(sum_ref, in_ref):
        out = sum_ref[y].astype(F32)
        for d in range(1, NY):
            out = out + in_ref[d - 1].astype(F32)
        return out

    whole = rng[...].reshape(rows_d, RANK)
    gp[...] = dot(whole, whole, 0, 0).reshape(gp.shape)
    s_g = scatter_core(gp, gcore)
    zp[...] = dot(whole, resid[...], 0, 0).astype(BF16).reshape(zp.shape)
    arrive(s_g)
    s_g = scatter_y(gp, gcore, gs, gy_in, F32)
    s_z = scatter_core(zp, zcore)
    for i in range(8):
        sl = slice(128 * i, 128 * i + 128)
        inv = 1.0 / scale[sl, 0:1]
        rscaled[sl, :] = (rng[i // 2, 4 * (i % 2):4 * (i % 2) + 4].reshape(128, RANK).astype(F32) * inv).astype(BF16)
    arrive(s_g)
    gfull[k, y] = owned(gs, gy_in)
    s_g = [send(gfull.at[k, y], gfull.at[k, y], dev(yy=yat(d))) for d in range(1, NY)]
    next(batch2)
    arrive(s_z)
    s_z = scatter_y(zp, zcore, zs, zy_in, BF16)
    for yy in range(NY):
        qp[sib, yy] = dot(cal[yy, sib * 4 + x], rscaled[...], 1, 0).astype(BF16)
    s_q = scatter_core(qp, qcore)
    for yy in range(NY):
        qp[k, yy] = dot(cal[yy, k * 4 + x], rscaled[...], 1, 0).astype(BF16)
    arrive(s_g)
    s_g = [send(gfull.at[k], gfull.at[k], dev(kk=sib))]
    arrive(s_q)
    s_q = scatter_y(qp, qcore, qs, qy_in, BF16)
    arrive(s_g)

    m_ref[:, :RANK] = gfull[...].reshape(RANK, RANK)
    ii = lax.broadcasted_iota(jnp.int32, (RANK, RANK), 0)
    jj = lax.broadcasted_iota(jnp.int32, (RANK, RANK), 1)
    m_ref[:, RANK:] = jnp.where(ii == jj, 1.0, 0.0)
    inverse_factor(m_ref, linv, 0, 2)
    arrive(s_z)
    zfull[k, y] = owned(zs, zy_in).astype(BF16)
    s_z = [send(zfull.at[k, y], zfull.at[k, y], dev(yy=yat(d))) for d in range(1, NY)]
    arrive(s_q)
    qfull[x] = owned(qs, qy_in)
    s_q = [send(qfull.at[x], qfull.at[x], dev(xx=xat(d))) for d in range(1, NX)]
    next(batch1)
    inverse_factor(m_ref, linv, 2, 5)
    arrive(s_z)
    s_z = [send(zfull.at[k], zfull.at[k], dev(kk=sib))]
    next(batch2)
    inverse_factor(m_ref, linv, 5, 8)
    store(linv, linv_out)

    store(atot, a_out)
    arrive(s_q)
    store(qfull, q_out)
    arrive(s_z)
    store(zfull, z_out)
    for copy in pending:
        copy.wait_send()
    for copy in stores:
        copy.wait()


def output_kernel(
    w_in, a_in, q_in, linv_in, rng_in, z_in, scale_in, tau_in, sparse_out, basis_out, coeffs_out, err_out,
    w_ref, a_ref, q_ref, linv_ref, rng_ref, z_ref, scale_ref, tau_ref, sparse_ref, basis_ref, coeffs_ref, err_ref, lsem,
):
    used = [0]

    def copy(src, dst):
        i = used[0]
        used[0] += 1
        out = pltpu.make_async_copy(src, dst, lsem.at[i])
        out.start()
        return out

    parts = 4
    n = w_ref.shape[0] // parts
    cut = [pl.ds(i * n, n) for i in range(parts)]
    small = [copy(tau_in, tau_ref), copy(scale_in, scale_ref)]
    loads_w = [copy(w_in.at[c], w_ref.at[c]) for c in cut]
    loads_b = [copy(linv_in, linv_ref), copy(rng_in, rng_ref)]
    load_z, load_q, load_a = copy(z_in, z_ref), copy(q_in, q_ref), copy(a_in, a_ref)
    for c in small:
        c.wait()
    tau = tau_ref[0:1, 0:1]
    stores = []
    for p in range(parts):
        loads_w[p].wait()

        def rows(i, carry, p=p):
            sl = pl.ds(pl.multiple_of(p * n + i * 32, 32), 32)
            sc = scale_ref[sl, :]
            for t in range(w_ref.shape[1] // 128):
                tl = pl.ds(128 * t, 128)
                scaled = sc * w_ref[sl, tl].astype(F32)
                sparse_ref[sl, tl] = (scaled - jnp.clip(scaled, -tau, tau)).astype(BF16)
            return carry

        lax.fori_loop(0, n // 32, rows, 0)
        stores.append(copy(sparse_ref.at[cut[p]], sparse_out.at[cut[p]]))
    for c in loads_b:
        c.wait()
    hi, lo = split2(linv_ref[...])
    pair = jnp.concatenate([hi, lo], axis=1)
    rng = rng_ref[...]
    basis_ref[...] = dot(jnp.concatenate([rng, rng], axis=1), pair, 1, 1).astype(BF16)
    stores.append(copy(basis_ref, basis_out))
    load_z.wait()
    zz = z_ref[...]
    coeffs = dot(pair, jnp.concatenate([zz, zz], axis=0), 1, 0).astype(BF16)
    coeffs_ref[...] = coeffs
    stores.append(copy(coeffs_ref, coeffs_out))
    load_q.wait()
    qh, ql = split2(q_ref[...])
    m = dot(jnp.concatenate([qh, qh, ql], axis=1), jnp.concatenate([hi, lo, hi], axis=1), 1, 1)
    mh, ml = split2(m)
    load_a.wait()
    err_ref[...] = a_ref[...] - dot(jnp.concatenate([mh, ml], axis=1), jnp.concatenate([coeffs, coeffs], axis=0), 1, 0)
    stores.append(copy(err_ref, err_out))
    for c in stores:
        c.wait()


def shards(weight, calib, sketch):
    d, f = weight.shape
    t = calib.shape[0]
    nrow = d // NX
    vm = pltpu.VMEM
    shape = jax.ShapeDtypeStruct
    out_shape = (
        shape((4, t, f), F32), shape((NX, t, RANK), F32), shape((RANK, RANK), F32), shape((NX, NZ, nrow // NZ, RANK), BF16),
        shape((2, NY, 32, f), BF16), shape((d, 128), F32), shape((8, 128), F32),
    )

    def scatter(n, width, kind):
        return [vm((2, NY, n, width), kind), vm((NY, n, width), kind), vm((NY, n, width), kind), vm((NY - 1, n, width), kind)]

    batches = (CUT, t - CUT)
    scratch = [
        vm((d, f), BF16), vm((f, RANK), BF16), vm((NX, NZ, t, d), BF16),
        vm((2, d), F32), vm((NX - 1, 2, d), F32), vm((2, d), F32), vm((NZ - 1, 2, d), F32),
        vm((8, 128), F32), vm((7, 8, 128), F32), vm((8, 128), F32), vm((d, 128), F32),
        vm((d, f), BF16), vm((d, f), BF16),
        vm((NX, nrow, RANK), BF16), vm((NX - 1, nrow, RANK), BF16),
        vm((NZ, nrow // NZ, RANK), BF16), vm((NZ - 1, nrow // NZ, RANK), BF16),
        vm((NX, NZ, nrow // NZ, RANK), BF16), vm((d, RANK), BF16),
        *scatter(32, RANK, F32), vm((2, NY, 32, RANK), F32),
        *scatter(32, f, BF16), vm((2, NY, 32, f), BF16),
        *scatter(t, RANK, BF16), vm((NX, t, RANK), F32),
        [vm((2, NY, 4 * n, f), BF16) for n in batches],
        [vm((NY, 4 * n, f), BF16) for n in batches],
        [vm((NY, 4 * n, f), BF16) for n in batches],
        [vm((2, 2 * n, f), BF16) for n in batches],
        [vm((2, 4 * n, f), BF16) for n in batches],
        vm((4, t, f), F32), vm((RANK, 2 * RANK), F32), vm((RANK, RANK), F32),
        pltpu.SemaphoreType.DMA((128,)), pltpu.SemaphoreType.DMA((128,)), pltpu.SemaphoreType.DMA((16,)),
    ]
    anywhere = pl.BlockSpec(memory_space=pl.ANY)
    a, q, linv, rng, zz, scale, tau = pl.pallas_call(
        exchange_kernel,
        out_shape=out_shape,
        in_specs=[anywhere] * 3,
        out_specs=[anywhere] * len(out_shape),
        scratch_shapes=scratch,
        compiler_params=pltpu.CompilerParams(collective_id=0, has_side_effects=True, vmem_limit_bytes=60 * 2**20),
    )(weight, calib, sketch)
    ins = (weight, a.reshape(NX * t, f), q.reshape(NX * t, RANK), linv, rng.reshape(d, RANK), zz.reshape(RANK, f), scale, tau)
    out_shape = (shape((d, f), BF16), shape((d, RANK), BF16), shape((RANK, f), BF16), shape((256, f), F32))
    return pl.pallas_call(
        output_kernel,
        out_shape=out_shape,
        in_specs=[anywhere] * 8,
        out_specs=[anywhere] * 4,
        scratch_shapes=[vm(v.shape, v.dtype) for v in (*ins, *out_shape)] + [pltpu.SemaphoreType.DMA((24,))],
        compiler_params=pltpu.CompilerParams(vmem_limit_bytes=60 * 2**20),
    )(*ins)


def solution(mesh):
    return jax.shard_map(
        shards,
        mesh=mesh,
        in_specs=(P("cols", "rows"), P("rows", "cols"), P("rows", None)),
        out_specs=(P("cols", "rows"), P("cols", None), P(None, "rows"), P("cols", "rows")),
        check_vma=False,
    )
```

```python
import jax
import jax.numpy as jnp
from jax import lax
from jax.experimental import pallas as pl
from jax.experimental.pallas import tpu as pltpu
from jax.sharding import PartitionSpec as P

MESH = pl.DeviceIdType.MESH
F32, BF16 = jnp.float32, jnp.bfloat16
NX, NZ, NY = 4, 8, 4
RANK = 256
PANEL = 32
CUT = 32


def split3(v):
    a = v.astype(BF16)
    rest = v - a.astype(F32)
    b = rest.astype(BF16)
    return a, b, (rest - b.astype(F32)).astype(BF16)


def split2(v):
    a = v.astype(BF16)
    return a, (v - a.astype(F32)).astype(BF16)


def dot(a, b, ca, cb):
    return lax.dot_general(a, b, (((ca,), (cb,)), ((), ())), preferred_element_type=F32)


def inverse_factor(m_ref, out_ref, start, stop):
    lane = lax.broadcasted_iota(jnp.int32, (PANEL, 2 * RANK), 1)
    sub8 = lax.broadcasted_iota(jnp.int32, (8, 128), 0)
    groups = PANEL // 8

    def panel(step, carry):
        k0 = pl.multiple_of(step * PANEL, PANEL)
        rows = m_ref[pl.ds(k0, PANEL), :]
        rows = jnp.where(lane >= k0, rows, 0.0)
        diag = pltpu.roll(rows[:, :RANK], lax.rem(RANK - k0, RANK), 1)[:, :128]
        rg = [rows[8 * g:8 * g + 8, :] for g in range(groups)]
        dg = [diag[8 * g:8 * g + 8, :] for g in range(groups)]
        for q in range(groups):
            left = range(groups - q)
            col = [
                [jnp.broadcast_to(dg[g][:, 8 * q + j:8 * q + j + 1], (8, 128)) for g in range(q, groups)]
                for j in range(8)
            ]
            pivots = jnp.zeros((8, 128), F32)
            for j in range(8):
                pivot = jnp.broadcast_to(col[j][0][j:j + 1, :], (8, 128))
                inv = 1.0 / pivot
                pivots = jnp.where(sub8 == j, pivot, pivots)
                mult = [col[j][g] * inv for g in left]
                mult[0] = jnp.where(sub8 > j, mult[0], 0.0)
                for other in range(j + 1, 8):
                    row = jnp.broadcast_to(col[other][0][j:j + 1, :], (8, 128))
                    for g in left:
                        col[other][g] = col[other][g] - mult[g] * row
                rrow, drow = rg[q][j:j + 1, :], dg[q][j:j + 1, :]
                for g in left:
                    rg[q + g] = rg[q + g] - jnp.concatenate([mult[g]] * 4, axis=1) * rrow
                    dg[q + g] = dg[q + g] - mult[g] * drow
            root = lax.rsqrt(pivots)
            rg[q] = rg[q] * jnp.concatenate([root] * 4, axis=1)
        done = jnp.concatenate(rg, axis=0)
        out_ref[pl.ds(k0, PANEL), :] = done[:, RANK:]
        a, b, c = split3(done)
        lhs = jnp.concatenate([a, a, b, a, b, c], axis=0)[:, :RANK]
        rhs = jnp.concatenate([a, b, a, c, b, a], axis=0)
        m_ref[...] -= dot(lhs, rhs, 0, 0)
        return carry

    lax.fori_loop(start, stop, panel, 0)


def exchange_kernel(
    w_in, cal_in, sk_in,
    a_out, q_out, linv_out, rng_out, z_out, scale_out, tau_out,
    w_ref, sk_ref, cal, stx, stx_in, stz, stz_in, tsend, t_in, tau_ref, scale, resid, rclip, rp, rx_in, rzs, rz_in, rng, rscaled,
    gp, gcore, gs, gy_in, gfull, zp, zcore, zs, zy_in, zfull, qp, qcore, qs, qy_in, qfull, ap, acore, asum, ay1, ay2, atot, m_ref, linv,
    ssem, rsem, lsem,
):
    rr, cc = lax.axis_index("rows"), lax.axis_index("cols")
    x, z = rr // NZ, lax.rem(rr, NZ)
    y, k = cc // 2, lax.rem(cc, 2)
    sib = 1 - k
    rows_d, cols_f = w_ref.shape

    def xat(d):
        return lax.rem(x + d, NX)

    def zat(d):
        return lax.rem(z + d, NZ)

    def yat(d):
        return lax.rem(y + d, NY)

    def dev(xx=x, zz=z, yy=y, kk=k):
        return (xx * NZ + zz, yy * 2 + kk)

    used = [0, 0]
    pending, stores = [], []

    def send(src, dst, to):
        i = used[0]
        used[0] += 1
        copy = pltpu.make_async_remote_copy(
            src_ref=src, dst_ref=dst, send_sem=ssem.at[i], recv_sem=rsem.at[i], device_id=to, device_id_type=MESH
        )
        copy.start()
        pending.append(copy)
        return copy

    def arrive(copies):
        for copy in copies:
            copy.wait_recv()

    def local(src, dst):
        i = used[1]
        used[1] += 1
        copy = pltpu.make_async_copy(src, dst, lsem.at[i])
        copy.start()
        return copy

    def store(src, dst):
        stores.append(local(src, dst))

    load_cal = local(cal_in, cal.at[x, z])
    load_w = local(w_in, w_ref)
    load_sk = local(sk_in, sk_ref)

    barrier = pltpu.get_barrier_semaphore()
    partners = [dev(xx=xat(d)) for d in range(1, NX)] + [dev(zz=zat(d)) for d in range(1, NZ)]
    partners += [(rr, lax.rem(cc + d, 8)) for d in range(1, 8)]
    for p in partners:
        pl.semaphore_signal(barrier, inc=1, device_id=p, device_id_type=MESH)

    load_cal.wait()
    for i in range(2):
        part = cal[x, z, :, 512 * i:512 * i + 512].astype(F32)
        stx[0:1, 512 * i:512 * i + 512] = jnp.sum(part * part, axis=0, keepdims=True)
    load_w.wait()
    ones = jnp.ones((8, cols_f), BF16)
    for i in range(4):
        stx[1:2, 256 * i:256 * i + 256] = dot(ones, jnp.abs(w_ref[256 * i:256 * i + 256, :]), 1, 1)[0:1, :]
    pl.semaphore_wait(barrier, len(partners))

    xp, xm, zp_, zm = xat(1), xat(NX - 1), zat(1), zat(NZ - 1)
    half = rows_d // 2
    lower, upper = pl.ds(0, half), pl.ds(half, half)
    first, second = pl.ds(0, CUT), pl.ds(CUT, 64 - CUT)

    def both(up, down, along):
        if along == 0:
            return [send(up, up, dev(xx=xp)), send(down, down, dev(xx=xm))]
        return [send(up, up, dev(zz=zp_)), send(down, down, dev(zz=zm))]

    def lane_first():
        copies = both(cal.at[x, z, first], cal.at[x, z, first], 0)
        yield
        arrive(copies)
        copies = both(cal.at[xm, z, first, lower], cal.at[xp, z, first, upper], 0)
        yield
        arrive(copies)
        for step in range(1, 5):
            part = (slice(None),) * 2 if step < 4 else (lower, upper)
            copies = both(cal.at[:, zat(NZ - step + 1), first, part[0]], cal.at[:, zat(step - 1), first, part[1]], 1)
            yield
            arrive(copies)
        yield

    def lane_second():
        for step in range(1, 5):
            part = (slice(None),) * 2 if step < 4 else (lower, upper)
            copies = both(cal.at[x, zat(NZ - step + 1), second, part[0]], cal.at[x, zat(step - 1), second, part[1]], 1)
            yield
            arrive(copies)
        copies = both(cal.at[x, :, second], cal.at[x, :, second], 0)
        yield
        arrive(copies)
        copies = both(cal.at[xm, :, second, lower], cal.at[xp, :, second, upper], 0)
        yield
        arrive(copies)
        yield

    lane1, lane2 = lane_first(), lane_second()

    sx = [send(stx, stx_in.at[d - 1], dev(xx=xat(d))) for d in range(1, NX)]
    next(lane1)
    next(lane2)
    arrive(sx)
    stz[...] = stx[...] + stx_in[0] + stx_in[1] + stx_in[2]
    sz = [send(stz, stz_in.at[d - 1], dev(zz=zat(d))) for d in range(1, NZ)]
    next(lane1)
    next(lane2)
    arrive(sz)
    tot = stz[...]
    for d in range(1, NZ):
        tot = tot + stz_in[d - 1]
    scale_row = jnp.sqrt(tot[0:1, :] / (NX * NZ * cal_in.shape[0]) + 1e-06)
    mine = jnp.sum(scale_row * tot[1:2, :], axis=1, keepdims=True)
    tsend[...] = jnp.broadcast_to(mine, (8, 128))
    st = [send(tsend, t_in.at[d - 1], (rr, lax.rem(cc + d, 8))) for d in range(1, 8)]
    next(lane1)
    next(lane2)
    for i in range(8):
        row = scale_row[:, 128 * i:128 * i + 128]
        scale[128 * i:128 * i + 128, :] = jnp.transpose(jnp.broadcast_to(row, (128, 128)))
    store(scale, scale_out)
    arrive(st)
    total = tsend[...]
    for d in range(1, 8):
        total = total + t_in[d - 1]
    tau_ref[...] = total * (2.0 / (float(rows_d * 8) * float(cols_f * NX * NZ)))
    store(tau_ref, tau_out)
    tau = tau_ref[0:1, 0:1]

    def clip_rows(i, carry):
        sl = pl.ds(pl.multiple_of(i * 32, 32), 32)
        sc = scale[sl, :]
        lim = tau / sc
        for t in range(cols_f // 128):
            tl = pl.ds(128 * t, 128)
            w = w_ref[sl, tl].astype(F32)
            resid[sl, tl] = jnp.clip(sc * w, -tau, tau).astype(BF16)
            rclip[sl, tl] = jnp.clip(w, -lim, lim).astype(BF16)
        return carry

    lax.fori_loop(0, rows_d // 64, clip_rows, 0)
    next(lane1)
    next(lane2)
    lax.fori_loop(rows_d // 64, rows_d // 32, clip_rows, 0)

    def scatter_core(part_ref, core_ref):
        return [send(part_ref.at[sib], core_ref, dev(kk=sib))]

    def lane_products(b, tokens, n):
        def fill(kk):
            for yy in range(NY):
                block = cal[yy, pl.ds(kk * 4, 4), tokens].reshape(4 * n, rows_d)
                ap[b][kk, yy] = dot(block, rclip[...], 1, 0).astype(BF16)

        fill(sib)
        copies = scatter_core(ap[b], acore[b])
        fill(k)
        yield
        arrive(copies)
        for yy in range(NY):
            asum[b][yy] = (ap[b][k, yy].astype(F32) + acore[b][yy].astype(F32)).astype(BF16)
        lo, hi = pl.ds(0, 2 * n), pl.ds(2 * n, 2 * n)
        yp, ym = yat(1), yat(NY - 1)
        copies = [send(asum[b].at[yat(2), lo], ay1[b].at[0], dev(yy=yp)), send(asum[b].at[yat(2), hi], ay1[b].at[1], dev(yy=ym))]
        yield
        arrive(copies)
        asum[b][yp, lo] = (asum[b][yp, lo].astype(F32) + ay1[b][0].astype(F32)).astype(BF16)
        asum[b][ym, hi] = (asum[b][ym, hi].astype(F32) + ay1[b][1].astype(F32)).astype(BF16)
        copies = [send(asum[b].at[yp], ay2[b].at[0], dev(yy=yp)), send(asum[b].at[ym], ay2[b].at[1], dev(yy=ym))]
        yield
        arrive(copies)
        whole = asum[b][y].astype(F32) + ay2[b][0].astype(F32) + ay2[b][1].astype(F32)
        atot[:, tokens, :] = whole.reshape(4, n, cols_f)
        yield

    batch1, batch2 = lane_products(0, first, CUT), lane_products(1, second, 64 - CUT)

    nrow = rows_d // NX
    load_sk.wait()
    sx = []
    for d in (2, 1, 3, 0):
        i = xat(d)
        rp[i] = dot(resid[pl.ds(pl.multiple_of(i * nrow, nrow), nrow), :], sk_ref[...], 1, 0).astype(BF16)
        if d:
            sx.append(send(rp.at[i], rx_in.at[d - 1], dev(xx=i)))
    next(lane1)
    next(lane2)
    arrive(sx)
    part = rp[x].astype(F32)
    for d in range(1, NX):
        part = part + rx_in[d - 1].astype(F32)
    rzs[...] = part.astype(BF16).reshape(NZ, nrow // NZ, RANK)
    sz = [send(rzs.at[zat(d)], rz_in.at[d - 1], dev(zz=zat(d))) for d in range(1, NZ)]
    next(lane1)
    arrive(sz)
    part = rzs[z].astype(F32)
    for d in range(1, NZ):
        part = part + rz_in[d - 1].astype(F32)
    rng[x, z] = part.astype(BF16)
    sz = [send(rng.at[x, z], rng.at[x, z], dev(zz=zat(d))) for d in range(1, NZ)]
    next(lane1)
    next(lane2)
    next(batch1)

    arrive(sz)
    sx = [send(rng.at[x], rng.at[x], dev(xx=xat(d))) for d in range(1, NX)]
    next(batch1)
    next(lane2)
    next(batch2)
    next(batch1)
    next(batch2)
    arrive(sx)
    store(rng, rng_out)

    def scatter_y(part_ref, core_ref, sum_ref, in_ref, kind):
        sum_ref[...] = (part_ref[k].astype(F32) + core_ref[...].astype(F32)).astype(kind)
        return [send(sum_ref.at[yat(d)], in_ref.at[d - 1], dev(yy=yat(d))) for d in range(1, NY)]

    def owned(sum_ref, in_ref):
        out = sum_ref[y].astype(F32)
        for d in range(1, NY):
            out = out + in_ref[d - 1].astype(F32)
        return out

    whole = rng[...].reshape(rows_d, RANK)
    gp[...] = dot(whole, whole, 0, 0).reshape(gp.shape)
    s_g = scatter_core(gp, gcore)
    zp[...] = dot(whole, resid[...], 0, 0).astype(BF16).reshape(zp.shape)
    arrive(s_g)
    s_g = scatter_y(gp, gcore, gs, gy_in, F32)
    s_z = scatter_core(zp, zcore)
    for i in range(8):
        sl = slice(128 * i, 128 * i + 128)
        inv = 1.0 / scale[sl, :]
        piece = rng[i // 2, 4 * (i % 2):4 * (i % 2) + 4].reshape(128, RANK).astype(F32)
        rscaled[sl, :] = (piece * jnp.concatenate([inv, inv], axis=1)).astype(BF16)
    arrive(s_g)
    gfull[k, y] = owned(gs, gy_in)
    s_g = [send(gfull.at[k, y], gfull.at[k, y], dev(yy=yat(d))) for d in range(1, NY)]
    next(batch2)
    arrive(s_z)
    s_z = scatter_y(zp, zcore, zs, zy_in, BF16)
    for yy in range(NY):
        qp[sib, yy] = dot(cal[yy, sib * 4 + x], rscaled[...], 1, 0).astype(BF16)
    s_q = scatter_core(qp, qcore)
    for yy in range(NY):
        qp[k, yy] = dot(cal[yy, k * 4 + x], rscaled[...], 1, 0).astype(BF16)
    arrive(s_g)
    s_g = [send(gfull.at[k], gfull.at[k], dev(kk=sib))]
    arrive(s_q)
    s_q = scatter_y(qp, qcore, qs, qy_in, BF16)
    arrive(s_g)

    m_ref[:, :RANK] = gfull[...].reshape(RANK, RANK)
    ii = lax.broadcasted_iota(jnp.int32, (RANK, RANK), 0)
    jj = lax.broadcasted_iota(jnp.int32, (RANK, RANK), 1)
    m_ref[:, RANK:] = jnp.where(ii == jj, 1.0, 0.0)
    inverse_factor(m_ref, linv, 0, 2)
    arrive(s_z)
    zfull[k, y] = owned(zs, zy_in).astype(BF16)
    s_z = [send(zfull.at[k, y], zfull.at[k, y], dev(yy=yat(d))) for d in range(1, NY)]
    arrive(s_q)
    qfull[x] = owned(qs, qy_in)
    s_q = [send(qfull.at[x], qfull.at[x], dev(xx=xat(d))) for d in range(1, NX)]
    inverse_factor(m_ref, linv, 2, 5)
    next(batch1)
    arrive(s_z)
    s_z = [send(zfull.at[k], zfull.at[k], dev(kk=sib))]
    inverse_factor(m_ref, linv, 5, 8)
    store(linv, linv_out)

    arrive(s_q)
    store(qfull, q_out)
    arrive(s_z)
    store(zfull, z_out)
    next(batch2)
    store(atot, a_out)
    for copy in pending:
        copy.wait_send()
    for copy in stores:
        copy.wait()


def output_kernel(
    w_in, a_in, q_in, linv_in, rng_in, z_in, scale_in, tau_in, sparse_out, basis_out, coeffs_out, err_out,
    w_ref, a_ref, q_ref, linv_ref, rng_ref, z_ref, scale_ref, tau_ref, sparse_ref, basis_ref, coeffs_ref, err_ref, lsem,
):
    used = [0]

    def copy(src, dst):
        i = used[0]
        used[0] += 1
        out = pltpu.make_async_copy(src, dst, lsem.at[i])
        out.start()
        return out

    parts = 4
    n = w_ref.shape[0] // parts
    cut = [pl.ds(i * n, n) for i in range(parts)]
    small = [copy(tau_in, tau_ref), copy(scale_in, scale_ref)]
    loads_w = [copy(w_in.at[c], w_ref.at[c]) for c in cut]
    loads_b = [copy(linv_in, linv_ref), copy(rng_in, rng_ref)]
    load_z, load_q, load_a = copy(z_in, z_ref), copy(q_in, q_ref), copy(a_in, a_ref)
    for c in small:
        c.wait()
    tau = tau_ref[0:1, 0:1]
    stores = []
    for p in range(parts):
        loads_w[p].wait()

        def rows(i, carry, p=p):
            sl = pl.ds(pl.multiple_of(p * n + i * 32, 32), 32)
            sc = scale_ref[sl, :]
            for t in range(w_ref.shape[1] // 128):
                tl = pl.ds(128 * t, 128)
                scaled = sc * w_ref[sl, tl].astype(F32)
                sparse_ref[sl, tl] = (scaled - jnp.clip(scaled, -tau, tau)).astype(BF16)
            return carry

        lax.fori_loop(0, n // 32, rows, 0)
        stores.append(copy(sparse_ref.at[cut[p]], sparse_out.at[cut[p]]))
    for c in loads_b:
        c.wait()
    hi, lo = split2(linv_ref[...])
    pair = jnp.concatenate([hi, lo], axis=1)
    rng = rng_ref[...]
    basis_ref[...] = dot(jnp.concatenate([rng, rng], axis=1), pair, 1, 1).astype(BF16)
    stores.append(copy(basis_ref, basis_out))
    load_z.wait()
    zz = z_ref[...]
    coeffs = dot(pair, jnp.concatenate([zz, zz], axis=0), 1, 0).astype(BF16)
    coeffs_ref[...] = coeffs
    stores.append(copy(coeffs_ref, coeffs_out))
    load_q.wait()
    qh, ql = split2(q_ref[...])
    m = dot(jnp.concatenate([qh, qh, ql], axis=1), jnp.concatenate([hi, lo, hi], axis=1), 1, 1)
    mh, ml = split2(m)
    load_a.wait()
    err_ref[...] = a_ref[...] - dot(jnp.concatenate([mh, ml], axis=1), jnp.concatenate([coeffs, coeffs], axis=0), 1, 0)
    stores.append(copy(err_ref, err_out))
    for c in stores:
        c.wait()


def shards(weight, calib, sketch):
    d, f = weight.shape
    t = calib.shape[0]
    nrow = d // NX
    vm = pltpu.VMEM
    shape = jax.ShapeDtypeStruct
    out_shape = (
        shape((4, t, f), F32), shape((NX, t, RANK), F32), shape((RANK, RANK), F32), shape((NX, NZ, nrow // NZ, RANK), BF16),
        shape((2, NY, 32, f), BF16), shape((d, 128), F32), shape((8, 128), F32),
    )

    def scatter(n, width, kind):
        return [vm((2, NY, n, width), kind), vm((NY, n, width), kind), vm((NY, n, width), kind), vm((NY - 1, n, width), kind)]

    batches = (CUT, t - CUT)
    scratch = [
        vm((d, f), BF16), vm((f, RANK), BF16), vm((NX, NZ, t, d), BF16),
        vm((2, d), F32), vm((NX - 1, 2, d), F32), vm((2, d), F32), vm((NZ - 1, 2, d), F32),
        vm((8, 128), F32), vm((7, 8, 128), F32), vm((8, 128), F32), vm((d, 128), F32),
        vm((d, f), BF16), vm((d, f), BF16),
        vm((NX, nrow, RANK), BF16), vm((NX - 1, nrow, RANK), BF16),
        vm((NZ, nrow // NZ, RANK), BF16), vm((NZ - 1, nrow // NZ, RANK), BF16),
        vm((NX, NZ, nrow // NZ, RANK), BF16), vm((d, RANK), BF16),
        *scatter(32, RANK, F32), vm((2, NY, 32, RANK), F32),
        *scatter(32, f, BF16), vm((2, NY, 32, f), BF16),
        *scatter(t, RANK, BF16), vm((NX, t, RANK), F32),
        [vm((2, NY, 4 * n, f), BF16) for n in batches],
        [vm((NY, 4 * n, f), BF16) for n in batches],
        [vm((NY, 4 * n, f), BF16) for n in batches],
        [vm((2, 2 * n, f), BF16) for n in batches],
        [vm((2, 4 * n, f), BF16) for n in batches],
        vm((4, t, f), F32), vm((RANK, 2 * RANK), F32), vm((RANK, RANK), F32),
        pltpu.SemaphoreType.DMA((128,)), pltpu.SemaphoreType.DMA((128,)), pltpu.SemaphoreType.DMA((16,)),
    ]
    anywhere = pl.BlockSpec(memory_space=pl.ANY)
    a, q, linv, rng, zz, scale, tau = pl.pallas_call(
        exchange_kernel,
        out_shape=out_shape,
        in_specs=[anywhere] * 3,
        out_specs=[anywhere] * len(out_shape),
        scratch_shapes=scratch,
        compiler_params=pltpu.CompilerParams(collective_id=0, has_side_effects=True, vmem_limit_bytes=60 * 2**20),
    )(weight, calib, sketch)
    ins = (weight, a.reshape(NX * t, f), q.reshape(NX * t, RANK), linv, rng.reshape(d, RANK), zz.reshape(RANK, f), scale, tau)
    out_shape = (shape((d, f), BF16), shape((d, RANK), BF16), shape((RANK, f), BF16), shape((256, f), F32))
    return pl.pallas_call(
        output_kernel,
        out_shape=out_shape,
        in_specs=[anywhere] * 8,
        out_specs=[anywhere] * 4,
        scratch_shapes=[vm(v.shape, v.dtype) for v in (*ins, *out_shape)] + [pltpu.SemaphoreType.DMA((24,))],
        compiler_params=pltpu.CompilerParams(vmem_limit_bytes=60 * 2**20),
    )(*ins)


def solution(mesh):
    return jax.shard_map(
        shards,
        mesh=mesh,
        in_specs=(P("cols", "rows"), P("rows", "cols"), P("rows", None)),
        out_specs=(P("cols", "rows"), P("cols", None), P(None, "rows"), P("cols", "rows")),
        check_vma=False,
    )
```
